32 devices in a mesh: blk: 2 (over x), grp: 16 (over z, y, core).
Axes of the slice: x: 2, y: 2, z: 4, core: 2. Of those that a mesh axis runs over, the one named last changes fastest.
Arguments:
- images: bfloat16 [512, 1152], P(('blk', 'grp')), may hold values from -6 to 6
- texts: bfloat16 [512, 1152], P(('blk', 'grp')), may hold values from -6 to 6
- scale: float32 [], replicated, may hold values from 8 to 16
- shift: float32 [], replicated, may hold values from -5 to -3
Outputs:
- image_loss: float32 [512], P(('blk', 'grp'))
- image_grad: float32 [512, 1152], P(('blk', 'grp'))
- text_grad: float32 [512, 1152], P(('blk', 'grp'))
The draws below stay inside these ranges and needn't reach their ends.
All inputs are finite; a program needn't handle non-finite values.
Results may differ from the reference program's by a relative error of at most 0.0045.
Values may be sent and summed in bfloat16 or wider, within the bound.
No kernel may reach another device: no remote copies, remote signals or barrier semaphores. Data moves between devices by JAX's collectives and lax.ppermute only.
A program may use at most 64 MiB of HBM per device.

```python
import jax
import jax.numpy as jnp
from jax import lax

D = 1152
BATCH = 512


def level_of(stream_key, extent, split, smallest, top_value):
    def one(position, parts):
        draws = jax.random.uniform(jax.random.fold_in(jax.random.fold_in(stream_key, 6), position), (parts,), jnp.float32, smallest / len(split), top_value / len(split))
        return jnp.repeat(jnp.exp(draws), extent[position] // parts).reshape((-1,) + (1,) * (len(extent) - position - 1))

    level = one(*split[0])
    for cut in split[1:]:
        level = level * one(*cut)
    return level


def bell_draw(key, extent, scale, limit, cuts=(), kind=jnp.bfloat16):
    drawn = jax.random.normal(key, extent, jnp.float32) * scale
    if len(cuts) > 0:
        drawn = level_of(key, extent, cuts, -0.22, 0.18) * drawn
    return jnp.clip(drawn, min=-limit, max=limit).astype(kind)


def setup_inputs(seed: int = 0) -> dict:
    streams_of = jax.random.split(jax.random.key(seed), 5)
    return {
        "images": bell_draw(streams_of[0], (BATCH, D), 1.0, 6.0, ((0, 32),)),
        "texts": bell_draw(streams_of[1], (BATCH, D), 1.0, 6.0, ((0, 32),)),
        "scale": jnp.clip(jax.random.uniform(streams_of[2], (), jnp.float32, 8.0, 16.0), 8.0, 16.0),
        "shift": jnp.clip(jax.random.uniform(streams_of[3], (), jnp.float32, -5.0, -3.0), -5.0, -3.0),
    }


def unit_rows(values):
    floats = values.astype(jnp.float32)
    norms = jnp.sqrt(lax.optimization_barrier(jnp.sum(floats * floats, 1, keepdims=True)) + 1e-06)
    return (floats / norms, norms)

def back_rows(grads, units, norms):
    return (grads - units * lax.optimization_barrier(jnp.sum(units * grads, 1, keepdims=True))) / norms

def reference(images, texts, scale, shift):
    image_unit, image_norm = unit_rows(images)
    text_unit, text_norm = unit_rows(texts)
    image_emb = image_unit.astype(jnp.bfloat16)
    text_emb = text_unit.astype(jnp.bfloat16)
    total = images.shape[0]
    width = 512 if total % 512 == 0 else total
    count = total // width
    blocks = image_emb.reshape(count, width, -1)

    def step(carry, item):
        block, index = item
        logit = scale * lax.dot_general(block, text_emb, (((1,), (1,)), ((), ())), preferred_element_type=jnp.float32) + shift
        rows_ids = index * width + jnp.arange(width, dtype=jnp.int32)[:, None]
        cols_ids = jnp.arange(total, dtype=jnp.int32)[None, :]
        label = (rows_ids == cols_ids).astype(jnp.float32)
        loss = lax.optimization_barrier(jnp.sum(jax.nn.softplus(logit * (1.0 - 2.0 * label)), 1)) / total
        coef = ((jax.nn.sigmoid(logit) - label) * scale).astype(jnp.bfloat16)
        grad_image = jnp.dot(coef, text_emb, preferred_element_type=jnp.float32)
        carry = carry + lax.dot_general(coef, block, (((0,), (0,)), ((), ())), preferred_element_type=jnp.float32)
        return (carry, (loss, grad_image))
    start = jnp.zeros((total, images.shape[1]), jnp.float32)
    text_sum, (losses, image_sum) = lax.scan(step, start, (blocks, jnp.arange(count, dtype=jnp.int32)))
    image_grad = back_rows(image_sum.reshape(total, -1), image_unit, image_norm)
    text_grad = back_rows(text_sum, text_unit, text_norm)
    return (losses.reshape(total), image_grad, text_grad)
```

```python
import functools

import jax
import jax.numpy as jnp
from jax import lax
from jax.experimental import pallas as pl
from jax.experimental.pallas import tpu as pltpu
from jax.sharding import PartitionSpec as P

AXES = ("blk", "grp")
LANES = 128
VMEM_BYTES = 24 * 1024 * 1024


def spread(value, bits):
    return sum(bit for place, bit in enumerate(bits) if value >> place & 1)


def plan(blocks, groups):
    bits = [1 << place for place in range((blocks * groups).bit_length() - 1)][1:]
    half = len(bits) // 2
    top = [bit for bit in bits if bit >= groups]
    low = [bit for bit in bits if bit < groups]
    need = half - len(top)
    image_bits = low[:need] + top
    text_bits = low[need:]
    order = sorted(
        range(1, 1 << half), key=lambda k: -bin(k).count("1")
    )
    return [(spread(k, image_bits), spread(k, text_bits)) for k in order]


def permuted(value, devices, image_step, text_step):
    pairs = [(d, d ^ (text_step if d & 1 else image_step)) for d in range(devices)]
    return lax.ppermute(value, AXES, pairs)


def first_core():
    return lax.axis_index("grp") % 2 == 0


def units(values):
    floats = values.astype(jnp.float32)
    norms = jnp.sqrt(jnp.sum(floats * floats, 1, keepdims=True) + 1e-06)
    return floats / norms, norms


def embed_kernel(images, texts, keep, send):
    image_emb = units(images[...])[0].astype(jnp.bfloat16)
    text_emb = units(texts[...])[0].astype(jnp.bfloat16)
    first = first_core()

    @pl.when(first)
    def _():
        keep[...] = image_emb
        send[...] = text_emb

    @pl.when(jnp.logical_not(first))
    def _():
        keep[...] = text_emb
        send[...] = image_emb


def tile_kernel(rows, total, scale_ref, shift_ref, mine, other, *outs):
    scale = scale_ref[0]
    shift = shift_ref[0]
    own = mine[...]
    far = other[...]
    count = own.shape[0]
    size = 2 * rows
    nt = (((1,), (1,)), ((), ()))
    row = lax.broadcasted_iota(jnp.int32, (count, count), 0)
    column = lax.broadcasted_iota(jnp.int32, (count, count), 1)
    hit = jnp.logical_and(row == column, row < size)
    label = hit.astype(jnp.float32)
    logit = scale * lax.dot_general(own, far, nt, preferred_element_type=jnp.float32) + shift
    coef = ((jax.nn.sigmoid(logit) - label) * scale).astype(jnp.bfloat16)
    grad = jnp.dot(coef, far, preferred_element_type=jnp.float32)
    turned = scale * lax.dot_general(far, own, nt, preferred_element_type=jnp.float32) + shift
    signed = turned * (1.0 - 2.0 * label)
    soft = jnp.maximum(signed, 0.0) + jnp.log1p(jnp.exp(-jnp.abs(signed)))
    loss = jnp.sum(soft, 0, keepdims=True) / total
    chunks = own.shape[1] // LANES
    for slot, out in enumerate(outs):
        for core in range(2):
            top = slot * size + core * rows
            for chunk in range(chunks):
                at = (core * chunks + chunk) * rows
                out[at : at + rows, :] = grad[top : top + rows, chunk * LANES : (chunk + 1) * LANES]
        lane = slot * size
        part = loss[:, lane // LANES * LANES : lane // LANES * LANES + LANES]
        part = jnp.broadcast_to(part, (8, LANES))
        if lane % LANES:
            part = pltpu.roll(part, LANES - lane % LANES, 1)
        out[2 * chunks * rows :, :] = part


def finish_kernel(images, texts, kept, came, loss_out, image_out, text_out):
    rows, width = images.shape
    chunks = width // LANES
    first = first_core()

    def back(raw, grads):
        unit, norm = units(raw[...])
        grad = jnp.concatenate(
            [grads[chunk * rows : (chunk + 1) * rows, :] for chunk in range(chunks)], 1
        )
        return (grad - unit * jnp.sum(unit * grad, 1, keepdims=True)) / norm

    @pl.when(first)
    def _():
        loss_out[...] = kept[chunks * rows : chunks * rows + 1, :]
        image_out[...] = back(images, kept)
        text_out[...] = back(texts, came)

    @pl.when(jnp.logical_not(first))
    def _():
        loss_out[...] = pltpu.roll(came[chunks * rows :, :], LANES - rows, 1)[:1]
        image_out[...] = back(images, came)
        text_out[...] = back(texts, kept)


def vmem(count):
    return [pl.BlockSpec(memory_space=pltpu.VMEM)] * count


def local(images, texts, scale, shift, blocks, groups):
    rows, width = images.shape
    devices = blocks * groups
    params = pltpu.CompilerParams(vmem_limit_bytes=VMEM_BYTES)
    steps = plan(blocks, groups)
    chunks = width // LANES
    first = first_core()
    piece = jax.ShapeDtypeStruct((rows, width), jnp.bfloat16)
    keep, send = pl.pallas_call(
        embed_kernel,
        out_shape=(piece, piece),
        in_specs=vmem(2),
        out_specs=tuple(vmem(2)),
        compiler_params=params,
        name="embed",
    )(images, texts)
    got = permuted(send, devices, 1, 1)
    chip = jnp.where(first, jnp.concatenate([keep, got], 0), jnp.concatenate([got, keep], 0))
    gathered = [permuted(chip, devices, a, b) for a, b in reversed(steps)][::-1]
    mine = jnp.concatenate([chip] + gathered, 0)
    other = permuted(mine, devices, 1, 1)
    message = jax.ShapeDtypeStruct((2 * chunks * rows + 8, LANES), jnp.float32)
    parts = pl.pallas_call(
        functools.partial(tile_kernel, rows, devices * rows),
        out_shape=[message] * (len(steps) + 1),
        in_specs=[pl.BlockSpec(memory_space=pltpu.SMEM)] * 2 + vmem(2),
        out_specs=vmem(len(steps) + 1),
        compiler_params=params,
        name="tile",
    )(scale.reshape(1), shift.reshape(1), mine, other)
    arrived = [permuted(part, devices, a, b) for part, (a, b) in zip(parts[1:], steps)]
    whole = parts[0]
    for part in arrived:
        whole = whole + part
    half = chunks * rows
    upper, lower, tail = whole[:half], whole[half : 2 * half], whole[2 * half :]
    kept = jnp.concatenate([jnp.where(first, upper, lower), tail], 0)
    leaving = jnp.concatenate([jnp.where(first, lower, upper), tail], 0)
    came = permuted(leaving, devices, 1, 1)
    loss, image_grad, text_grad = pl.pallas_call(
        finish_kernel,
        out_shape=(
            jax.ShapeDtypeStruct((1, LANES), jnp.float32),
            jax.ShapeDtypeStruct((rows, width), jnp.float32),
            jax.ShapeDtypeStruct((rows, width), jnp.float32),
        ),
        in_specs=vmem(4),
        out_specs=tuple(vmem(3)),
        compiler_params=params,
        name="finish",
    )(images, texts, kept, came)
    return loss[0, :rows], image_grad, text_grad


def solution(mesh):
    in_specs = (P(AXES, None), P(AXES, None), P(), P())
    out_specs = (P(AXES), P(AXES, None), P(AXES, None))
    step = functools.partial(local, blocks=mesh.shape["blk"], groups=mesh.shape["grp"])
    return jax.shard_map(step, mesh=mesh, in_specs=in_specs, out_specs=out_specs, check_vma=False)
```

```python
import functools

import jax
import jax.numpy as jnp
from jax import lax
from jax.experimental import pallas as pl
from jax.experimental.pallas import tpu as pltpu
from jax.sharding import PartitionSpec as P

AXES = ("blk", "grp")
LANES = 128
SCALE_TOP = 16.0
FLOAT16_TOP = 65504.0
VMEM_BYTES = 24 * 1024 * 1024


def spread(value, bits):
    return sum(bit for place, bit in enumerate(bits) if value >> place & 1)


def plan(blocks, groups):
    bits = [1 << place for place in range((blocks * groups).bit_length() - 1)][1:]
    half = len(bits) // 2
    top = [bit for bit in bits if bit >= groups]
    low = [bit for bit in bits if bit < groups]
    need = half - len(top)
    image_bits = low[:need] + top
    text_bits = low[need:]
    return [
        (spread(k, image_bits), spread(k ^ k >> 1, text_bits)) for k in range(1, 1 << half)
    ]


def permuted(value, devices, image_step, text_step):
    pairs = [(d, d ^ (text_step if d & 1 else image_step)) for d in range(devices)]
    return lax.ppermute(value, AXES, pairs)


def first_core():
    return lax.axis_index("grp") % 2 == 0


def message_lift(count):
    lift = 1.0
    while lift * 2 * count * SCALE_TOP < FLOAT16_TOP:
        lift *= 2
    return lift


def units(values):
    floats = values.astype(jnp.float32)
    norms = jnp.sqrt(jnp.sum(floats * floats, 1, keepdims=True) + 1e-06)
    return floats / norms, norms


def embed_kernel(own, images_near, texts_near, chip):
    rows = own.shape[0]

    def embed(raw):
        return units(raw[...])[0].astype(jnp.bfloat16)

    first = first_core()

    @pl.when(first)
    def _():
        chip[:rows, :] = embed(own)
        chip[rows:, :] = embed(images_near)

    @pl.when(jnp.logical_not(first))
    def _():
        chip[:rows, :] = embed(texts_near)
        chip[rows:, :] = embed(own)


def tile_kernel(rows, scale_ref, shift_ref, mine, other, *outs):
    scale = scale_ref[0]
    shift = shift_ref[0]
    own = mine[...]
    far = other[...]
    count = own.shape[0]
    size = 2 * rows
    nt = (((1,), (1,)), ((), ()))
    row = lax.broadcasted_iota(jnp.int32, (count, count), 0)
    column = lax.broadcasted_iota(jnp.int32, (count, count), 1)
    hit = jnp.logical_and(row == column, row < size)
    label = hit.astype(jnp.float32)
    logit = scale * lax.dot_general(own, far, nt, preferred_element_type=jnp.float32) + shift
    coef = ((jax.nn.sigmoid(logit) - label) * scale).astype(jnp.bfloat16)
    grad = jnp.dot(coef, far, preferred_element_type=jnp.float32)
    turned = scale * lax.dot_general(far, own, nt, preferred_element_type=jnp.float32) + shift
    signed = turned * (1.0 - 2.0 * label)
    soft = jnp.maximum(signed, 0.0) + jnp.log1p(jnp.exp(-jnp.abs(signed)))
    loss = jnp.sum(soft, 0, keepdims=True)
    chunks = own.shape[1] // LANES
    for slot, out in enumerate(outs):
        for core in range(2):
            top = slot * size + core * rows
            for chunk in range(chunks):
                at = (core * chunks + chunk) * rows
                out[at : at + rows, :] = grad[top : top + rows, chunk * LANES : (chunk + 1) * LANES]
        lane = slot * size
        part = loss[:, lane // LANES * LANES : lane // LANES * LANES + LANES]
        part = jnp.broadcast_to(part, (8, LANES))
        if lane % LANES:
            part = pltpu.roll(part, LANES - lane % LANES, 1)
        out[2 * chunks * rows :, :] = part


def finish_kernel(total, images, texts, kept, came, loss_out, image_out, text_out):
    rows, width = images.shape
    chunks = width // LANES
    first = first_core()

    def back(raw, grads):
        unit, norm = units(raw[...])
        grad = jnp.concatenate(
            [grads[chunk * rows : (chunk + 1) * rows, :] for chunk in range(chunks)], 1
        )
        return (grad - unit * jnp.sum(unit * grad, 1, keepdims=True)) / norm

    @pl.when(first)
    def _():
        loss_out[...] = kept[chunks * rows, :rows] / total
        image_out[...] = back(images, kept)
        text_out[...] = back(texts, came)

    @pl.when(jnp.logical_not(first))
    def _():
        loss_out[...] = pltpu.roll(came[chunks * rows :, :], LANES - rows, 1)[0, :rows] / total
        image_out[...] = back(images, came)
        text_out[...] = back(texts, kept)


def vmem(count):
    return [pl.BlockSpec(memory_space=pltpu.VMEM)] * count


def local(images, texts, scale, shift, blocks, groups):
    rows, width = images.shape
    devices = blocks * groups
    params = pltpu.CompilerParams(vmem_limit_bytes=VMEM_BYTES)
    steps = plan(blocks, groups)
    chunks = width // LANES
    first = first_core()
    images_near = permuted(images, devices, 1, 1)
    texts_near = permuted(texts, devices, 1, 1)
    chip = pl.pallas_call(
        embed_kernel,
        out_shape=jax.ShapeDtypeStruct((2 * rows, width), jnp.bfloat16),
        in_specs=vmem(3),
        out_specs=vmem(1)[0],
        compiler_params=params,
        name="embed",
    )(jnp.where(first, images, texts), images_near, texts_near)
    gathered = [permuted(chip, devices, a, b) for a, b in steps]
    mine = jnp.concatenate([chip] + gathered, 0)
    other = permuted(mine, devices, 1, 1)
    message = jax.ShapeDtypeStruct((2 * chunks * rows + 8, LANES), jnp.float32)
    parts = pl.pallas_call(
        functools.partial(tile_kernel, rows),
        out_shape=[message] * (len(steps) + 1),
        in_specs=[pl.BlockSpec(memory_space=pltpu.SMEM)] * 2 + vmem(2),
        out_specs=vmem(len(steps) + 1),
        compiler_params=params,
        name="tile",
    )(scale.reshape(1), shift.reshape(1), mine, other)
    lift = message_lift(2 * rows << len(steps).bit_length())
    whole = parts[0]
    for part, (a, b) in zip(parts[1:], steps):
        sent = (part * lift).astype(jnp.float16)
        whole = whole + permuted(sent, devices, a, b).astype(jnp.float32) * (1.0 / lift)
    half = chunks * rows
    upper, lower, tail = whole[:half], whole[half : 2 * half], whole[2 * half :]
    kept = jnp.concatenate([jnp.where(first, upper, lower), tail], 0)
    leaving = jnp.concatenate([jnp.where(first, lower, upper), tail], 0)
    came = permuted(leaving, devices, 1, 1)
    loss, image_grad, text_grad = pl.pallas_call(
        functools.partial(finish_kernel, devices * rows),
        out_shape=(
            jax.ShapeDtypeStruct((rows,), jnp.float32),
            jax.ShapeDtypeStruct((rows, width), jnp.float32),
            jax.ShapeDtypeStruct((rows, width), jnp.float32),
        ),
        in_specs=vmem(4),
        out_specs=tuple(vmem(3)),
        compiler_params=params,
        name="finish",
    )(images, texts, kept, came)
    return loss, image_grad, text_grad


def solution(mesh):
    in_specs = (P(AXES, None), P(AXES, None), P(), P())
    out_specs = (P(AXES), P(AXES, None), P(AXES, None))
    step = functools.partial(local, blocks=mesh.shape["blk"], groups=mesh.shape["grp"])
    return jax.shard_map(step, mesh=mesh, in_specs=in_specs, out_specs=out_specs, check_vma=False)
```

```python
import functools

import jax
import jax.numpy as jnp
from jax import lax
from jax.experimental import pallas as pl
from jax.experimental.pallas import tpu as pltpu
from jax.sharding import PartitionSpec as P

AXES = ("blk", "grp")
LANES = 128
SCALE_TOP = 16.0
FLOAT16_TOP = 65504.0
VMEM_BYTES = 24 * 1024 * 1024


def spread(value, bits):
    return sum(bit for place, bit in enumerate(bits) if value >> place & 1)


def plan(blocks, groups):
    bits = [1 << place for place in range((blocks * groups).bit_length() - 1)][1:]
    half = len(bits) // 2
    top = [bit for bit in bits if bit >= groups]
    low = [bit for bit in bits if bit < groups]
    need = half - len(top)
    image_bits = top + low[:need]
    text_bits = low[need:]
    return [(spread(k, image_bits), spread(k, text_bits)) for k in range(1, 1 << half)]


def permuted(value, devices, image_step, text_step):
    pairs = [(d, d ^ (text_step if d & 1 else image_step)) for d in range(devices)]
    return lax.ppermute(value, AXES, pairs)


def first_core():
    return lax.axis_index("grp") % 2 == 0


def message_lift(count):
    lift = 1.0
    while lift * 2 * count * SCALE_TOP < FLOAT16_TOP:
        lift *= 2
    return lift


def units(values):
    floats = values.astype(jnp.float32)
    norms = jnp.sqrt(jnp.sum(floats * floats, 1, keepdims=True) + 1e-06)
    return floats / norms, norms


def embed_kernel(own, images_near, texts_near, chip):
    rows = own.shape[0]

    def embed(raw):
        return units(raw[...])[0].astype(jnp.bfloat16)

    first = first_core()

    @pl.when(first)
    def _():
        chip[:rows, :] = embed(own)
        chip[rows:, :] = embed(images_near)

    @pl.when(jnp.logical_not(first))
    def _():
        chip[:rows, :] = embed(texts_near)
        chip[rows:, :] = embed(own)


def tile_kernel(rows, scale_ref, shift_ref, mine, other, *outs):
    scale = scale_ref[0]
    shift = shift_ref[0]
    own = mine[...]
    far = other[...]
    count = own.shape[0]
    size = 2 * rows
    nt = (((1,), (1,)), ((), ()))
    row = lax.broadcasted_iota(jnp.int32, (count, count), 0)
    column = lax.broadcasted_iota(jnp.int32, (count, count), 1)
    hit = jnp.logical_and(row == column, row < size)
    label = hit.astype(jnp.float32)
    logit = scale * lax.dot_general(own, far, nt, preferred_element_type=jnp.float32) + shift
    coef = ((jax.nn.sigmoid(logit) - label) * scale).astype(jnp.bfloat16)
    grad = jnp.dot(coef, far, preferred_element_type=jnp.float32)
    signed = logit * (1.0 - 2.0 * label)
    soft = jnp.maximum(signed, 0.0) + jnp.log1p(jnp.exp(-jnp.abs(signed)))
    loss = jnp.sum(soft.T, 0, keepdims=True)
    chunks = own.shape[1] // LANES
    for slot, out in enumerate(outs):
        for core in range(2):
            top = slot * size + core * rows
            for chunk in range(chunks):
                at = (core * chunks + chunk) * rows
                out[at : at + rows, :] = grad[top : top + rows, chunk * LANES : (chunk + 1) * LANES]
        lane = slot * size
        part = loss[:, lane // LANES * LANES : lane // LANES * LANES + LANES]
        part = jnp.broadcast_to(part, (8, LANES))
        if lane % LANES:
            part = pltpu.roll(part, LANES - lane % LANES, 1)
        out[2 * chunks * rows :, :] = part


def finish_kernel(total, images, texts, kept, came, loss_out, image_out, text_out):
    rows, width = images.shape
    chunks = width // LANES
    first = first_core()

    def back(raw, grads):
        unit, norm = units(raw[...])
        grad = jnp.concatenate(
            [grads[chunk * rows : (chunk + 1) * rows, :] for chunk in range(chunks)], 1
        )
        return (grad - unit * jnp.sum(unit * grad, 1, keepdims=True)) / norm

    @pl.when(first)
    def _():
        loss_out[...] = kept[chunks * rows, :rows] / total
        image_out[...] = back(images, kept)
        text_out[...] = back(texts, came)

    @pl.when(jnp.logical_not(first))
    def _():
        loss_out[...] = pltpu.roll(came[chunks * rows :, :], LANES - rows, 1)[0, :rows] / total
        image_out[...] = back(images, came)
        text_out[...] = back(texts, kept)


def vmem(count):
    return [pl.BlockSpec(memory_space=pltpu.VMEM)] * count


def local(images, texts, scale, shift, blocks, groups):
    rows, width = images.shape
    devices = blocks * groups
    params = pltpu.CompilerParams(vmem_limit_bytes=VMEM_BYTES)
    steps = plan(blocks, groups)
    chunks = width // LANES
    first = first_core()
    images_near = permuted(images, devices, 1, 1)
    texts_near = permuted(texts, devices, 1, 1)
    chip = pl.pallas_call(
        embed_kernel,
        out_shape=jax.ShapeDtypeStruct((2 * rows, width), jnp.bfloat16),
        in_specs=vmem(3),
        out_specs=vmem(1)[0],
        compiler_params=params,
        name="embed",
    )(jnp.where(first, images, texts), images_near, texts_near)
    gathered = [permuted(chip, devices, a, b) for a, b in steps]
    mine = jnp.concatenate([chip] + gathered, 0)
    other = permuted(mine, devices, 1, 1)
    message = jax.ShapeDtypeStruct((2 * chunks * rows + 8, LANES), jnp.float32)
    parts = pl.pallas_call(
        functools.partial(tile_kernel, rows),
        out_shape=[message] * (len(steps) + 1),
        in_specs=[pl.BlockSpec(memory_space=pltpu.SMEM)] * 2 + vmem(2),
        out_specs=vmem(len(steps) + 1),
        compiler_params=params,
        name="tile",
    )(scale.reshape(1), shift.reshape(1), mine, other)
    lift = message_lift(2 * rows << len(steps).bit_length())
    whole = parts[0]
    for part, (a, b) in zip(parts[1:], steps):
        sent = (part * lift).astype(jnp.float16)
        whole = whole + permuted(sent, devices, a, b).astype(jnp.float32) * (1.0 / lift)
    half = chunks * rows
    upper, lower, tail = whole[:half], whole[half : 2 * half], whole[2 * half :]
    kept = jnp.concatenate([jnp.where(first, upper, lower), tail], 0)
    leaving = jnp.concatenate([jnp.where(first, lower, upper), tail], 0)
    came = permuted(leaving, devices, 1, 1)
    loss, image_grad, text_grad = pl.pallas_call(
        functools.partial(finish_kernel, devices * rows),
        out_shape=(
            jax.ShapeDtypeStruct((rows,), jnp.float32),
            jax.ShapeDtypeStruct((rows, width), jnp.float32),
            jax.ShapeDtypeStruct((rows, width), jnp.float32),
        ),
        in_specs=vmem(4),
        out_specs=tuple(vmem(3)),
        compiler_params=params,
        name="finish",
    )(images, texts, kept, came)
    return loss, image_grad, text_grad


def solution(mesh):
    in_specs = (P(AXES, None), P(AXES, None), P(), P())
    out_specs = (P(AXES), P(AXES, None), P(AXES, None))
    step = functools.partial(local, blocks=mesh.shape["blk"], groups=mesh.shape["grp"])
    return jax.shard_map(step, mesh=mesh, in_specs=in_specs, out_specs=out_specs, check_vma=False)
```

```python
import functools

import jax
import jax.numpy as jnp
from jax import lax
from jax.experimental import pallas as pl
from jax.experimental.pallas import tpu as pltpu
from jax.sharding import PartitionSpec as P

AXES = ("blk", "grp")
LANES = 128
SCALE_TOP = 16.0
FLOAT16_TOP = 65504.0
VMEM_BYTES = 24 * 1024 * 1024


def spread(value, bits):
    return sum(bit for place, bit in enumerate(bits) if value >> place & 1)


def plan(blocks, groups):
    bits = [1 << place for place in range((blocks * groups).bit_length() - 1)][1:]
    half = len(bits) // 2
    top = [bit for bit in bits if bit >= groups]
    low = [bit for bit in bits if bit < groups]
    need = half - len(top)
    image_bits = low[:need] + top
    text_bits = low[need:]
    last = (1 << half) - 1
    return [(spread(k, image_bits), spread(k, text_bits)) for k in [last, *range(1, last)]]


def permuted(value, devices, image_step, text_step):
    pairs = [(d, d ^ (text_step if d & 1 else image_step)) for d in range(devices)]
    return lax.ppermute(value, AXES, pairs)


def first_core():
    return lax.axis_index("grp") % 2 == 0


def message_lift(count):
    lift = 1.0
    while lift * 2 * count * SCALE_TOP < FLOAT16_TOP:
        lift *= 2
    return lift


def units(values):
    floats = values.astype(jnp.float32)
    norms = jnp.sqrt(jnp.sum(floats * floats, 1, keepdims=True) + 1e-06)
    return floats / norms, norms


def embed_kernel(flip, own, images_near, texts_near, chip):
    rows = images_near.shape[0]

    def place(upper, lower):
        chip[:rows, :] = units(upper)[0].astype(jnp.bfloat16)
        chip[rows:, :] = units(lower)[0].astype(jnp.bfloat16)

    first = first_core()
    images, texts = own[:rows, :], own[rows:, :]

    @pl.when(first)
    def _():
        place(*((texts, texts_near[...]) if flip else (images, images_near[...])))

    @pl.when(jnp.logical_not(first))
    def _():
        place(*((images_near[...], images) if flip else (texts_near[...], texts)))


def tile_kernel(rows, scale_ref, shift_ref, mine, other, *outs):
    scale = scale_ref[0]
    shift = shift_ref[0]
    own = mine[...]
    far = other[...]
    count = own.shape[0]
    size = 2 * rows
    nt = (((1,), (1,)), ((), ()))
    row = lax.broadcasted_iota(jnp.int32, (count, count), 0)
    column = lax.broadcasted_iota(jnp.int32, (count, count), 1)
    hit = jnp.logical_and(row == column, row < size)
    label = hit.astype(jnp.float32)
    logit = scale * lax.dot_general(own, far, nt, preferred_element_type=jnp.float32) + shift
    coef = ((jax.nn.sigmoid(logit) - label) * scale).astype(jnp.bfloat16)
    grad = jnp.dot(coef, far, preferred_element_type=jnp.float32)
    signed = logit * (1.0 - 2.0 * label)
    soft = jnp.maximum(signed, 0.0) + jnp.log1p(jnp.exp(-jnp.abs(signed)))
    loss = jnp.sum(soft.T, 0, keepdims=True)
    chunks = own.shape[1] // LANES
    for slot, out in enumerate(outs):
        for core in range(2):
            top = slot * size + core * rows
            for chunk in range(chunks):
                at = (core * chunks + chunk) * rows
                out[at : at + rows, :] = grad[top : top + rows, chunk * LANES : (chunk + 1) * LANES]
        lane = slot * size
        part = loss[:, lane // LANES * LANES : lane // LANES * LANES + LANES]
        part = jnp.broadcast_to(part, (8, LANES))
        if lane % LANES:
            part = pltpu.roll(part, LANES - lane % LANES, 1)
        out[2 * chunks * rows :, :] = part


def finish_kernel(total, images, texts, kept, came, loss_out, image_out, text_out):
    rows, width = images.shape
    chunks = width // LANES
    first = first_core()

    def back(raw, grads):
        unit, norm = units(raw[...])
        grad = jnp.concatenate(
            [grads[chunk * rows : (chunk + 1) * rows, :] for chunk in range(chunks)], 1
        )
        return (grad - unit * jnp.sum(unit * grad, 1, keepdims=True)) / norm

    @pl.when(first)
    def _():
        loss_out[...] = kept[chunks * rows, :rows] / total
        image_out[...] = back(images, kept)
        text_out[...] = back(texts, came)

    @pl.when(jnp.logical_not(first))
    def _():
        loss_out[...] = pltpu.roll(came[chunks * rows :, :], LANES - rows, 1)[0, :rows] / total
        image_out[...] = back(images, came)
        text_out[...] = back(texts, kept)


def vmem(count):
    return [pl.BlockSpec(memory_space=pltpu.VMEM)] * count


def local(images, texts, scale, shift, blocks, groups):
    rows, width = images.shape
    devices = blocks * groups
    params = pltpu.CompilerParams(vmem_limit_bytes=VMEM_BYTES)
    steps = plan(blocks, groups)
    chunks = width // LANES
    first = first_core()
    images_near = permuted(images, devices, 1, 1)
    texts_near = permuted(texts, devices, 1, 1)
    own = jnp.concatenate([images, texts], 0)
    chip, chip_other = [
        pl.pallas_call(
            functools.partial(embed_kernel, flip),
            out_shape=jax.ShapeDtypeStruct((2 * rows, width), jnp.bfloat16),
            in_specs=vmem(3),
            out_specs=vmem(1)[0],
            compiler_params=params,
            name=name,
        )(own, images_near, texts_near)
        for flip, name in ((False, "embed"), (True, "embed_other"))
    ]
    gathered = [permuted(chip, devices, a, b) for a, b in steps]
    mine = jnp.concatenate([chip] + gathered, 0)
    other = jnp.concatenate([chip_other] + [permuted(part, devices, 1, 1) for part in gathered], 0)
    message = jax.ShapeDtypeStruct((2 * chunks * rows + 8, LANES), jnp.float32)
    parts = pl.pallas_call(
        functools.partial(tile_kernel, rows),
        out_shape=[message] * (len(steps) + 1),
        in_specs=[pl.BlockSpec(memory_space=pltpu.SMEM)] * 2 + vmem(2),
        out_specs=vmem(len(steps) + 1),
        compiler_params=params,
        name="tile",
    )(scale.reshape(1), shift.reshape(1), mine, other)
    lift = message_lift(2 * rows << len(steps).bit_length())
    whole = parts[0]
    sends = list(zip(parts[1:], steps))
    for part, (a, b) in sends[1:] + sends[:1]:
        sent = (part * lift).astype(jnp.float16)
        whole = whole + permuted(sent, devices, a, b).astype(jnp.float32) * (1.0 / lift)
    half = chunks * rows
    upper, lower, tail = whole[:half], whole[half : 2 * half], whole[2 * half :]
    kept = jnp.concatenate([jnp.where(first, upper, lower), tail], 0)
    leaving = jnp.concatenate([jnp.where(first, lower, upper), tail], 0)
    came = permuted(leaving, devices, 1, 1)
    loss, image_grad, text_grad = pl.pallas_call(
        functools.partial(finish_kernel, devices * rows),
        out_shape=(
            jax.ShapeDtypeStruct((rows,), jnp.float32),
            jax.ShapeDtypeStruct((rows, width), jnp.float32),
            jax.ShapeDtypeStruct((rows, width), jnp.float32),
        ),
        in_specs=vmem(4),
        out_specs=tuple(vmem(3)),
        compiler_params=params,
        name="finish",
    )(images, texts, kept, came)
    return loss, image_grad, text_grad


def solution(mesh):
    in_specs = (P(AXES, None), P(AXES, None), P(), P())
    out_specs = (P(AXES), P(AXES, None), P(AXES, None))
    step = functools.partial(local, blocks=mesh.shape["blk"], groups=mesh.shape["grp"])
    return jax.shard_map(step, mesh=mesh, in_specs=in_specs, out_specs=out_specs, check_vma=False)
```

```python
import functools

import jax
import jax.numpy as jnp
from jax import lax
from jax.experimental import pallas as pl
from jax.experimental.pallas import tpu as pltpu
from jax.sharding import PartitionSpec as P

AXES = ("blk", "grp")
LANES = 128
SCALE_TOP = 16.0
FLOAT16_TOP = 65504.0
VMEM_BYTES = 24 * 1024 * 1024


def spread(value, bits):
    return sum(bit for place, bit in enumerate(bits) if value >> place & 1)


def plan(blocks, groups):
    bits = [1 << place for place in range((blocks * groups).bit_length() - 1)][1:]
    half = len(bits) // 2
    top = [bit for bit in bits if bit >= groups]
    low = [bit for bit in bits if bit < groups]
    need = half - len(top)
    image_bits = low[:need] + top
    text_bits = low[need:]
    last = (1 << half) - 1
    return [(spread(k, image_bits), spread(k, text_bits)) for k in [*range(last - 1, 0, -1), last]]


def permuted(value, devices, image_step, text_step):
    pairs = [(d, d ^ (text_step if d & 1 else image_step)) for d in range(devices)]
    return lax.ppermute(value, AXES, pairs)


def first_core():
    return lax.axis_index("grp") % 2 == 0


def message_lift(count):
    lift = 1.0
    while lift * 2 * count * SCALE_TOP < FLOAT16_TOP:
        lift *= 2
    return lift


def units(values):
    floats = values.astype(jnp.float32)
    norms = jnp.sqrt(jnp.sum(floats * floats, 1, keepdims=True) + 1e-06)
    return floats / norms, norms


def place(out, raw, near):
    rows = raw.shape[0]
    out[:rows, :] = units(raw)[0].astype(jnp.bfloat16)
    out[rows:, :] = units(near[...])[0].astype(jnp.bfloat16)


def by_core(takes_images, own, images_near, texts_near, out):
    rows = images_near.shape[0]

    @pl.when(takes_images)
    def _():
        place(out, own[:rows, :], images_near)

    @pl.when(jnp.logical_not(takes_images))
    def _():
        place(out, own[rows:, :], texts_near)


def embed_kernel(own, images_near, texts_near, chip):
    by_core(first_core(), own, images_near, texts_near, chip)


def embed_other_kernel(own, images_near, texts_near, chip, unit_out, norm_out):
    by_core(jnp.logical_not(first_core()), own, images_near, texts_near, chip)
    unit, norm = units(own[...])
    unit_out[...] = unit
    norm_out[...] = jnp.broadcast_to(norm, norm_out.shape)


def tile_kernel(rows, scale_ref, shift_ref, mine, other, *outs):
    scale = scale_ref[0]
    shift = shift_ref[0]
    own = mine[...]
    far = other[...]
    count = own.shape[0]
    size = 2 * rows
    nt = (((1,), (1,)), ((), ()))
    row = lax.broadcasted_iota(jnp.int32, (count, count), 0)
    column = lax.broadcasted_iota(jnp.int32, (count, count), 1)
    hit = jnp.logical_and(row == column, row < size)
    label = hit.astype(jnp.float32)
    logit = scale * lax.dot_general(own, far, nt, preferred_element_type=jnp.float32) + shift
    coef = ((jax.nn.sigmoid(logit) - label) * scale).astype(jnp.bfloat16)
    grad = jnp.dot(coef, far, preferred_element_type=jnp.float32)
    signed = logit * (1.0 - 2.0 * label)
    soft = jnp.maximum(signed, 0.0) + jnp.log1p(jnp.exp(-jnp.abs(signed)))
    loss = jnp.sum(soft.T, 0, keepdims=True)
    chunks = own.shape[1] // LANES
    half = chunks * rows + 8
    for slot, out in enumerate(outs):
        top = slot * size
        part = loss[:, top // LANES * LANES : top // LANES * LANES + LANES]
        part = jnp.broadcast_to(part, (8, LANES))
        if top % LANES:
            part = pltpu.roll(part, LANES - top % LANES, 1)
        for side in range(2):
            for chunk in range(chunks):
                at = side * half + chunk * rows
                out[at : at + rows, :] = grad[
                    top + side * rows : top + (side + 1) * rows, chunk * LANES : (chunk + 1) * LANES
                ]
            out[(side + 1) * half - 8 : (side + 1) * half, :] = part


def finish_kernel(total, unit, norm, kept, came, loss_out, image_out, text_out):
    rows, width = image_out.shape
    chunks = width // LANES
    at = chunks * rows

    def back(role, grads):
        own = unit[role * rows : (role + 1) * rows, :]
        grad = jnp.concatenate(
            [grads[chunk * rows : (chunk + 1) * rows, :] for chunk in range(chunks)], 1
        )
        flat = grad - own * jnp.sum(own * grad, 1, keepdims=True)
        return flat / norm[role * rows : (role + 1) * rows, :1]

    first = first_core()

    @pl.when(first)
    def _():
        image_out[...] = back(0, kept)
        text_out[...] = back(1, came)
        loss_out[...] = kept[at, :rows] / total

    @pl.when(jnp.logical_not(first))
    def _():
        image_out[...] = back(0, came)
        text_out[...] = back(1, kept)
        loss_out[...] = pltpu.roll(came[at:, :], LANES - rows, 1)[0, :rows] / total


def vmem(count):
    return [pl.BlockSpec(memory_space=pltpu.VMEM)] * count


def local(images, texts, scale, shift, blocks, groups):
    rows, width = images.shape
    devices = blocks * groups
    params = pltpu.CompilerParams(vmem_limit_bytes=VMEM_BYTES)
    steps = plan(blocks, groups)
    chunks = width // LANES
    images_near = permuted(images, devices, 1, 1)
    texts_near = permuted(texts, devices, 1, 1)
    own = jnp.concatenate([images, texts], 0)
    raws = (own, images_near, texts_near)
    piece = jax.ShapeDtypeStruct((2 * rows, width), jnp.bfloat16)
    chip = pl.pallas_call(
        embed_kernel,
        out_shape=piece,
        in_specs=vmem(3),
        out_specs=vmem(1)[0],
        compiler_params=params,
        name="embed",
    )(*raws)
    chip_other, unit, norm = pl.pallas_call(
        embed_other_kernel,
        out_shape=(
            piece,
            jax.ShapeDtypeStruct((2 * rows, width), jnp.float32),
            jax.ShapeDtypeStruct((2 * rows, LANES), jnp.float32),
        ),
        in_specs=vmem(3),
        out_specs=tuple(vmem(3)),
        compiler_params=params,
        name="embed_other",
    )(*raws)
    gathered = [permuted(chip, devices, a, b) for a, b in steps]
    slots = len(steps) + 1
    mine = jnp.concatenate([chip] + gathered, 0)
    other = jnp.concatenate([chip_other] + [permuted(part, devices, 1, 1) for part in gathered], 0)
    half = chunks * rows + 8
    message = jax.ShapeDtypeStruct((2 * half, LANES), jnp.float32)
    parts = pl.pallas_call(
        functools.partial(tile_kernel, rows),
        out_shape=[message] * slots,
        in_specs=[pl.BlockSpec(memory_space=pltpu.SMEM)] * 2 + vmem(2),
        out_specs=vmem(slots),
        compiler_params=params,
        name="tile",
    )(scale.reshape(1), shift.reshape(1), mine, other)
    lift = message_lift(2 * rows * slots)
    whole = parts[0]
    for part, (a, b) in zip(parts[1:], steps):
        sent = (part * lift).astype(jnp.float16)
        whole = whole + permuted(sent, devices, a, b).astype(jnp.float32) * (1.0 / lift)
    kept = whole[:half]
    came = permuted(whole[half:], devices, 1, 1)
    return pl.pallas_call(
        functools.partial(finish_kernel, devices * rows),
        out_shape=(
            jax.ShapeDtypeStruct((rows,), jnp.float32),
            jax.ShapeDtypeStruct((rows, width), jnp.float32),
            jax.ShapeDtypeStruct((rows, width), jnp.float32),
        ),
        in_specs=vmem(4),
        out_specs=tuple(vmem(3)),
        compiler_params=params,
        name="finish",
    )(unit, norm, kept, came)


def solution(mesh):
    in_specs = (P(AXES, None), P(AXES, None), P(), P())
    out_specs = (P(AXES), P(AXES, None), P(AXES, None))
    step = functools.partial(local, blocks=mesh.shape["blk"], groups=mesh.shape["grp"])
    return jax.shard_map(step, mesh=mesh, in_specs=in_specs, out_specs=out_specs, check_vma=False)
```

```python
import functools

import jax
import jax.numpy as jnp
from jax import lax
from jax.experimental import pallas as pl
from jax.experimental.pallas import tpu as pltpu
from jax.sharding import PartitionSpec as P

AXES = ("blk", "grp")
LANES = 128
SCALE_TOP = 16.0
FLOAT16_TOP = 65504.0
VMEM_BYTES = 24 * 1024 * 1024


def spread(value, bits):
    return sum(bit for place, bit in enumerate(bits) if value >> place & 1)


def plan(blocks, groups):
    bits = [1 << place for place in range((blocks * groups).bit_length() - 1)][1:]
    half = len(bits) // 2
    top = [bit for bit in bits if bit >= groups]
    low = [bit for bit in bits if bit < groups]
    need = half - len(top)
    image_bits = low[:need] + top
    text_bits = low[need:]
    last = (1 << half) - 1
    return [(spread(k, image_bits), spread(k, text_bits)) for k in [*range(last - 1, 0, -1), last]]


def permuted(value, devices, image_step, text_step):
    pairs = [(d, d ^ (text_step if d & 1 else image_step)) for d in range(devices)]
    return lax.ppermute(value, AXES, pairs)


def first_core():
    return lax.axis_index("grp") % 2 == 0


def message_lift(count):
    lift = 1.0
    while lift * 2 * count * SCALE_TOP < FLOAT16_TOP:
        lift *= 2
    return lift


def units(values):
    floats = values.astype(jnp.float32)
    norms = jnp.sqrt(jnp.sum(floats * floats, 1, keepdims=True) + 1e-06)
    return floats / norms, norms


def place(out, raw, near):
    rows = raw.shape[0]
    out[:rows, :] = units(raw)[0].astype(jnp.bfloat16)
    out[rows:, :] = units(near[...])[0].astype(jnp.bfloat16)


def by_core(takes_images, own, images_near, texts_near, out):
    rows = images_near.shape[0]

    @pl.when(takes_images)
    def _():
        place(out, own[:rows, :], images_near)

    @pl.when(jnp.logical_not(takes_images))
    def _():
        place(out, own[rows:, :], texts_near)


def embed_kernel(own, images_near, texts_near, chip):
    by_core(first_core(), own, images_near, texts_near, chip)


def embed_other_kernel(own, images_near, texts_near, chip, unit_out, norm_out):
    by_core(jnp.logical_not(first_core()), own, images_near, texts_near, chip)
    unit, norm = units(own[...])
    unit_out[...] = unit
    norm_out[...] = jnp.broadcast_to(norm, norm_out.shape)


def tile_kernel(rows, lift, scale_ref, shift_ref, mine, other, *outs):
    scale = scale_ref[0]
    shift = shift_ref[0]
    own = mine[...]
    far = other[...]
    count = own.shape[0]
    size = 2 * rows
    nt = (((1,), (1,)), ((), ()))
    row = lax.broadcasted_iota(jnp.int32, (count, count), 0)
    column = lax.broadcasted_iota(jnp.int32, (count, count), 1)
    hit = jnp.logical_and(row == column, row < size)
    label = hit.astype(jnp.float32)
    logit = scale * lax.dot_general(own, far, nt, preferred_element_type=jnp.float32) + shift
    coef = ((jax.nn.sigmoid(logit) - label) * scale).astype(jnp.bfloat16)
    grad = jnp.dot(coef, far, preferred_element_type=jnp.float32)
    signed = logit * (1.0 - 2.0 * label)
    soft = jnp.maximum(signed, 0.0) + jnp.log1p(jnp.exp(-jnp.abs(signed)))
    loss = jnp.sum(soft.T, 0, keepdims=True)
    chunks = own.shape[1] // LANES
    half = chunks * rows + 8
    for slot, out in enumerate(outs):
        top = slot * size
        part = loss[:, top // LANES * LANES : top // LANES * LANES + LANES]
        part = jnp.broadcast_to(part, (8, LANES)) * (lift if slot else 1.0)
        if top % LANES:
            part = pltpu.roll(part, LANES - top % LANES, 1)
        for side in range(2):
            for chunk in range(chunks):
                at = side * half + chunk * rows
                out[at : at + rows, :] = (lift if slot else 1.0) * grad[
                    top + side * rows : top + (side + 1) * rows, chunk * LANES : (chunk + 1) * LANES
                ]
            out[(side + 1) * half - 8 : (side + 1) * half, :] = part


def finish_kernel(total, unit, norm, kept, came, loss_out, image_out, text_out):
    rows, width = image_out.shape
    chunks = width // LANES
    at = chunks * rows

    def back(role, grads):
        own = unit[role * rows : (role + 1) * rows, :]
        grad = jnp.concatenate(
            [grads[chunk * rows : (chunk + 1) * rows, :] for chunk in range(chunks)], 1
        )
        flat = grad - own * jnp.sum(own * grad, 1, keepdims=True)
        return flat / norm[role * rows : (role + 1) * rows, :1]

    first = first_core()

    @pl.when(first)
    def _():
        image_out[...] = back(0, kept)
        text_out[...] = back(1, came)
        loss_out[...] = kept[at, :rows] / total

    @pl.when(jnp.logical_not(first))
    def _():
        image_out[...] = back(0, came)
        text_out[...] = back(1, kept)
        loss_out[...] = pltpu.roll(came[at:, :], LANES - rows, 1)[0, :rows] / total


def vmem(count):
    return [pl.BlockSpec(memory_space=pltpu.VMEM)] * count


def local(images, texts, scale, shift, blocks, groups):
    rows, width = images.shape
    devices = blocks * groups
    params = pltpu.CompilerParams(vmem_limit_bytes=VMEM_BYTES)
    steps = plan(blocks, groups)
    chunks = width // LANES
    images_near = permuted(images, devices, 1, 1)
    texts_near = permuted(texts, devices, 1, 1)
    own = jnp.concatenate([images, texts], 0)
    raws = (own, images_near, texts_near)
    piece = jax.ShapeDtypeStruct((2 * rows, width), jnp.bfloat16)
    chip = pl.pallas_call(
        embed_kernel,
        out_shape=piece,
        in_specs=vmem(3),
        out_specs=vmem(1)[0],
        compiler_params=params,
        name="embed",
    )(*raws)
    chip_other, unit, norm = pl.pallas_call(
        embed_other_kernel,
        out_shape=(
            piece,
            jax.ShapeDtypeStruct((2 * rows, width), jnp.float32),
            jax.ShapeDtypeStruct((2 * rows, LANES), jnp.float32),
        ),
        in_specs=vmem(3),
        out_specs=tuple(vmem(3)),
        compiler_params=params,
        name="embed_other",
    )(*raws)
    gathered = [permuted(chip, devices, a, b) for a, b in steps]
    slots = len(steps) + 1
    mine = jnp.concatenate([chip] + gathered, 0)
    other = jnp.concatenate([chip_other] + [permuted(part, devices, 1, 1) for part in gathered], 0)
    half = chunks * rows + 8
    lift = message_lift(2 * rows * slots)
    message = jax.ShapeDtypeStruct((2 * half, LANES), jnp.float32)
    parts = pl.pallas_call(
        functools.partial(tile_kernel, rows, lift),
        out_shape=[message] * slots,
        in_specs=[pl.BlockSpec(memory_space=pltpu.SMEM)] * 2 + vmem(2),
        out_specs=vmem(slots),
        compiler_params=params,
        name="tile",
    )(scale.reshape(1), shift.reshape(1), mine, other)
    arrived = [permuted(part.astype(jnp.float16), devices, a, b) for part, (a, b) in zip(parts[1:], steps)]

    def total(span):
        return sum((part[span].astype(jnp.float32) * (1.0 / lift) for part in arrived), parts[0][span])

    came = permuted(total(slice(half, 2 * half)), devices, 1, 1)
    kept = total(slice(0, half))
    return pl.pallas_call(
        functools.partial(finish_kernel, devices * rows),
        out_shape=(
            jax.ShapeDtypeStruct((rows,), jnp.float32),
            jax.ShapeDtypeStruct((rows, width), jnp.float32),
            jax.ShapeDtypeStruct((rows, width), jnp.float32),
        ),
        in_specs=vmem(4),
        out_specs=tuple(vmem(3)),
        compiler_params=params,
        name="finish",
    )(unit, norm, kept, came)


def solution(mesh):
    in_specs = (P(AXES, None), P(AXES, None), P(), P())
    out_specs = (P(AXES), P(AXES, None), P(AXES, None))
    step = functools.partial(local, blocks=mesh.shape["blk"], groups=mesh.shape["grp"])
    return jax.shard_map(step, mesh=mesh, in_specs=in_specs, out_specs=out_specs, check_vma=False)
```

```python
import functools

import jax
import jax.numpy as jnp
from jax import lax
from jax.experimental import pallas as pl
from jax.experimental.pallas import tpu as pltpu
from jax.sharding import PartitionSpec as P

AXES = ("blk", "grp")
LANES = 128
SCALE_TOP = 16.0
FLOAT16_TOP = 65504.0
VMEM_BYTES = 24 * 1024 * 1024


def spread(value, bits):
    return sum(bit for place, bit in enumerate(bits) if value >> place & 1)


def plan(blocks, groups):
    bits = [1 << place for place in range((blocks * groups).bit_length() - 1)][1:]
    half = len(bits) // 2
    top = [bit for bit in bits if bit >= groups]
    low = [bit for bit in bits if bit < groups]
    need = half - len(top)
    image_bits = low[:need] + top
    text_bits = low[need:]
    last = (1 << half) - 1
    return [(spread(k, image_bits), spread(k, text_bits)) for k in [*range(last - 1, 0, -1), last]]


def permuted(value, devices, image_step, text_step, cross=0):
    pairs = [(d, d ^ (text_step if d & 1 else image_step) ^ cross) for d in range(devices)]
    return lax.ppermute(value, AXES, pairs)


def first_core():
    return lax.axis_index("grp") % 2 == 0


def message_lift(count):
    lift = 1.0
    while lift * 2 * count * SCALE_TOP < FLOAT16_TOP:
        lift *= 2
    return lift


def units(values):
    floats = values.astype(jnp.float32)
    norms = jnp.sqrt(jnp.sum(floats * floats, 1, keepdims=True) + 1e-06)
    return floats / norms, norms


def place(out, raw, near):
    rows = raw.shape[0]
    out[:rows, :] = units(raw)[0].astype(jnp.bfloat16)
    out[rows:, :] = units(near[...])[0].astype(jnp.bfloat16)


def by_core(takes_images, own, images_near, texts_near, out):
    rows = images_near.shape[0]

    @pl.when(takes_images)
    def _():
        place(out, own[:rows, :], images_near)

    @pl.when(jnp.logical_not(takes_images))
    def _():
        place(out, own[rows:, :], texts_near)


def embed_kernel(own, images_near, texts_near, chip):
    by_core(first_core(), own, images_near, texts_near, chip)


def embed_other_kernel(own, images_near, texts_near, chip, unit_out, norm_out):
    by_core(jnp.logical_not(first_core()), own, images_near, texts_near, chip)
    unit, norm = units(own[...])
    unit_out[...] = unit
    norm_out[...] = jnp.broadcast_to(norm, norm_out.shape)


def tile_kernel(rows, lift, scale_ref, shift_ref, mine, other, *outs):
    scale = scale_ref[0]
    shift = shift_ref[0]
    top = mine.shape[0] - 2 * rows
    own = jnp.concatenate([mine[:top, :], other[top:, :]], 0)
    far = jnp.concatenate([other[:top, :], mine[top:, :]], 0)
    count = own.shape[0]
    size = 2 * rows
    nt = (((1,), (1,)), ((), ()))
    row = lax.broadcasted_iota(jnp.int32, (count, count), 0)
    column = lax.broadcasted_iota(jnp.int32, (count, count), 1)
    hit = jnp.logical_and(row == column, row < size)
    label = hit.astype(jnp.float32)
    logit = scale * lax.dot_general(own, far, nt, preferred_element_type=jnp.float32) + shift
    coef = ((jax.nn.sigmoid(logit) - label) * scale).astype(jnp.bfloat16)
    grad = jnp.dot(coef, far, preferred_element_type=jnp.float32)
    signed = logit * (1.0 - 2.0 * label)
    soft = jnp.maximum(signed, 0.0) + jnp.log1p(jnp.exp(-jnp.abs(signed)))
    loss = jnp.sum(soft.T, 0, keepdims=True)
    chunks = own.shape[1] // LANES
    half = chunks * rows + 8
    for slot, out in enumerate(outs):
        top = slot * size
        part = loss[:, top // LANES * LANES : top // LANES * LANES + LANES]
        part = jnp.broadcast_to(part, (8, LANES)) * (lift if slot else 1.0)
        if top % LANES:
            part = pltpu.roll(part, LANES - top % LANES, 1)
        for side in range(2):
            for chunk in range(chunks):
                at = side * half + chunk * rows
                out[at : at + rows, :] = (lift if slot else 1.0) * grad[
                    top + side * rows : top + (side + 1) * rows, chunk * LANES : (chunk + 1) * LANES
                ]
            out[(side + 1) * half - 8 : (side + 1) * half, :] = part


def finish_kernel(total, unit, norm, kept, came, loss_out, image_out, text_out):
    rows, width = image_out.shape
    chunks = width // LANES
    at = chunks * rows

    def back(role, grads):
        own = unit[role * rows : (role + 1) * rows, :]
        grad = jnp.concatenate(
            [grads[chunk * rows : (chunk + 1) * rows, :] for chunk in range(chunks)], 1
        )
        flat = grad - own * jnp.sum(own * grad, 1, keepdims=True)
        return flat / norm[role * rows : (role + 1) * rows, :1]

    first = first_core()

    @pl.when(first)
    def _():
        image_out[...] = back(0, kept)
        text_out[...] = back(1, came)
        loss_out[...] = kept[at, :rows] / total

    @pl.when(jnp.logical_not(first))
    def _():
        image_out[...] = back(0, came)
        text_out[...] = back(1, kept)
        loss_out[...] = pltpu.roll(came[at:, :], LANES - rows, 1)[0, :rows] / total


def vmem(count):
    return [pl.BlockSpec(memory_space=pltpu.VMEM)] * count


def local(images, texts, scale, shift, blocks, groups):
    rows, width = images.shape
    devices = blocks * groups
    params = pltpu.CompilerParams(vmem_limit_bytes=VMEM_BYTES)
    steps = plan(blocks, groups)
    chunks = width // LANES
    images_near = permuted(images, devices, 1, 1)
    texts_near = permuted(texts, devices, 1, 1)
    own = jnp.concatenate([images, texts], 0)
    raws = (own, images_near, texts_near)
    piece = jax.ShapeDtypeStruct((2 * rows, width), jnp.bfloat16)
    chip = pl.pallas_call(
        embed_kernel,
        out_shape=piece,
        in_specs=vmem(3),
        out_specs=vmem(1)[0],
        compiler_params=params,
        name="embed",
    )(*raws)
    chip_other, unit, norm = pl.pallas_call(
        embed_other_kernel,
        out_shape=(
            piece,
            jax.ShapeDtypeStruct((2 * rows, width), jnp.float32),
            jax.ShapeDtypeStruct((2 * rows, LANES), jnp.float32),
        ),
        in_specs=vmem(3),
        out_specs=tuple(vmem(3)),
        compiler_params=params,
        name="embed_other",
    )(*raws)
    gathered = [permuted(chip, devices, a, b, int((a, b) == steps[-1])) for a, b in steps]
    slots = len(steps) + 1
    mine = jnp.concatenate([chip] + gathered, 0)
    other = jnp.concatenate([chip_other] + [permuted(part, devices, 1, 1) for part in gathered], 0)
    half = chunks * rows + 8
    lift = message_lift(2 * rows * slots)
    message = jax.ShapeDtypeStruct((2 * half, LANES), jnp.float32)
    parts = pl.pallas_call(
        functools.partial(tile_kernel, rows, lift),
        out_shape=[message] * slots,
        in_specs=[pl.BlockSpec(memory_space=pltpu.SMEM)] * 2 + vmem(2),
        out_specs=vmem(slots),
        compiler_params=params,
        name="tile",
    )(scale.reshape(1), shift.reshape(1), mine, other)
    arrived = [permuted(part.astype(jnp.float16), devices, a, b) for part, (a, b) in zip(parts[1:], steps)]

    def total(span):
        return sum((part[span].astype(jnp.float32) * (1.0 / lift) for part in arrived), parts[0][span])

    came = permuted(total(slice(half, 2 * half)), devices, 1, 1)
    kept = total(slice(0, half))
    return pl.pallas_call(
        functools.partial(finish_kernel, devices * rows),
        out_shape=(
            jax.ShapeDtypeStruct((rows,), jnp.float32),
            jax.ShapeDtypeStruct((rows, width), jnp.float32),
            jax.ShapeDtypeStruct((rows, width), jnp.float32),
        ),
        in_specs=vmem(4),
        out_specs=tuple(vmem(3)),
        compiler_params=params,
        name="finish",
    )(unit, norm, kept, came)


def solution(mesh):
    in_specs = (P(AXES, None), P(AXES, None), P(), P())
    out_specs = (P(AXES), P(AXES, None), P(AXES, None))
    step = functools.partial(local, blocks=mesh.shape["blk"], groups=mesh.shape["grp"])
    return jax.shard_map(step, mesh=mesh, in_specs=in_specs, out_specs=out_specs, check_vma=False)
```
